32 devices in a mesh: dp: 16 (over z, y, core), code: 2 (over x).
Axes of the slice: x: 2, y: 2, z: 4, core: 2. Of those that a mesh axis runs over, the one named last changes fastest.
Arguments:
- encoded: bfloat16 [4096, 256], P('dp'), may hold values from -32 to 32
- codebook: bfloat16 [131072, 256], P('code'), may hold values from -2 to 2
Outputs:
- grad_rows: float32 [4096, 256], P('dp')
- grad_codes: float32 [131072, 256], P(('code', 'dp'))
The draws below stay inside these ranges and needn't reach their ends.
All inputs are finite; a program needn't handle non-finite values.
Results may differ from the reference program's by a relative error of at most 0.0045.
Values may be sent and summed in bfloat16 or wider, within the bound.
No kernel may reach another device: no remote copies, remote signals or barrier semaphores. Data moves between devices by JAX's collectives and lax.ppermute only.
A program may use at most 128 MiB of HBM per device.

```python
import math
import jax
import jax.numpy as jnp
from jax import lax

D = 256
CODES = 131072
ROWS = 4096


def common_codebook(key):
    values = jax.random.normal(jax.random.fold_in(key, 7), (CODES, D), jnp.float32) * 0.25
    return jnp.clip(values, -2.0, 2.0)


def draw_codebook(key, part):
    return common_codebook(key).astype(jnp.bfloat16)


def draw_encoded(key, part):
    enc_key = jax.random.fold_in(key, 11)
    code_table = common_codebook(key)
    values = jax.random.normal(enc_key, (ROWS, D), jnp.float32)
    chosen = jax.random.randint(jax.random.fold_in(enc_key, 3), (12,), 0, ROWS)
    earlier = jax.random.randint(jax.random.fold_in(enc_key, 4), (12,), 0, CODES)
    later = jax.random.randint(jax.random.fold_in(enc_key, 5), (12,), 0, CODES)
    strength = jnp.tile(jnp.array([20.0, 26.0, 32.0], jnp.float32), 4)
    aligned = strength[:, None] * jnp.tanh(4.0 * (code_table[earlier] + code_table[later]))
    values = values.at[chosen].set(aligned)
    return jnp.clip(values, -32.0, 32.0).astype(jnp.bfloat16)


def setup_inputs(seed: int = 0) -> dict:
    streams_of = jax.random.split(jax.random.key(seed), 3)
    return {
        "encoded": draw_encoded(jax.random.fold_in(streams_of[2], 71), 0),
        "codebook": draw_codebook(jax.random.fold_in(streams_of[2], 71), 0),
    }


def logit_block(encoded, code_rows, code_squares):
    scores = lax.dot_general(encoded, code_rows, (((1,), (1,)), ((), ())), preferred_element_type=jnp.float32)
    return scores - 0.5 * code_squares[None, :]


def grad_block(encoded, row_lse, entropy, cross_term, code_rows, code_squares, log_mass):
    logits = logit_block(encoded, code_rows, code_squares)
    weights = jnp.exp(logits - row_lse[:, None])
    shaped = weights * (row_lse[:, None] - logits - entropy[:, None] + log_mass[None, :] - cross_term[:, None])
    return shaped.astype(jnp.bfloat16)


def code_term(grad_tile, encoded, code_rows):
    pulled = lax.dot_general(grad_tile, encoded, (((0,), (0,)), ((), ())), preferred_element_type=jnp.float32)
    totals = jnp.sum(grad_tile.astype(jnp.float32), axis=0)
    return pulled - totals[:, None] * code_rows.astype(jnp.float32)


def reference(encoded, codebook):
    squares = jnp.sum(jnp.square(codebook.astype(jnp.float32)), axis=1)
    block_size = math.gcd(CODES, 4096)
    block_count = CODES // block_size
    code_blocks = codebook.reshape(block_count, block_size, D)
    square_blocks = squares.reshape(block_count, block_size)

    def max_of(inputs):
        return jnp.max(logit_block(encoded, inputs[0], inputs[1]), axis=1)

    row_max = jnp.max(lax.map(max_of, (code_blocks, square_blocks)), axis=0)

    def sums_of(inputs):
        logits = logit_block(encoded, inputs[0], inputs[1])
        exponent = jnp.exp(logits - row_max[:, None])
        return jnp.sum(exponent, axis=1), jnp.sum(exponent * logits, axis=1)

    block_sums, block_dots = lax.map(sums_of, (code_blocks, square_blocks))
    row_sum = jnp.sum(block_sums, axis=0)
    row_dot = jnp.sum(block_dots, axis=0)
    row_lse = row_max + jnp.log(row_sum)
    entropy = row_lse - row_dot / row_sum

    def mass_of(inputs):
        logits = logit_block(encoded, inputs[0], inputs[1])
        return jnp.sum(jnp.exp(logits - row_lse[:, None]), axis=0)

    mean_mass = lax.map(mass_of, (code_blocks, square_blocks)).reshape(CODES) / ROWS
    log_mass = jnp.log(mean_mass)
    log_blocks = log_mass.reshape(block_count, block_size)

    def cross_of(inputs):
        logits = logit_block(encoded, inputs[0], inputs[1])
        weights = jnp.exp(logits - row_lse[:, None])
        return jnp.sum(weights * inputs[2][None, :], axis=1)

    cross_term = jnp.sum(lax.map(cross_of, (code_blocks, square_blocks, log_blocks)), axis=0)

    def grad_step(running, inputs):
        grad_tile = grad_block(encoded, row_lse, entropy, cross_term, inputs[0], inputs[1], inputs[2])
        added = running + jnp.dot(grad_tile, inputs[0], preferred_element_type=jnp.float32)
        return added, code_term(grad_tile, encoded, inputs[0])

    grad_rows, terms = lax.scan(grad_step, jnp.zeros((ROWS, D), jnp.float32), (code_blocks, square_blocks, log_blocks))
    return grad_rows, terms.reshape(CODES, D)
```

```python
import math

import jax
import jax.numpy as jnp
from jax import lax
from jax.experimental import pallas as pl
from jax.experimental.pallas import tpu as pltpu
from jax.sharding import PartitionSpec as P

LOG2E = math.log2(math.e)
LN2 = math.log(2.0)
LOG2LN2 = math.log2(LN2)
LANES = 128
PARAMS = pltpu.CompilerParams(vmem_limit_bytes=56 * 2**20)
NT = (((1,), (1,)), ((), ()))


def half_squares(code_rows):
    values = code_rows.astype(jnp.float32)
    return jnp.sum(values * values, axis=1, keepdims=True) * (0.5 * LOG2E)


def column_to_row(column):
    wide = jnp.broadcast_to(column, (column.shape[0], LANES))
    return jnp.transpose(wide)[0:1, :]


def stats_call(encoded_t, codebook):
    features, rows = encoded_t.shape
    codes = codebook.shape[0]
    block = math.gcd(codes, 8192)
    chunk = math.gcd(block, 256)

    def kernel(encoded_ref, codes_ref, max_ref, sum_ref, top, total):
        step = pl.program_id(0)

        @pl.when(step == 0)
        def _():
            top[...] = jnp.full(top.shape, -3e38, jnp.float32)
            total[...] = jnp.zeros(total.shape, jnp.float32)

        run_max, run_sum = top[...], total[...]
        for k in range(block // chunk):
            code_rows = codes_ref[k * chunk : (k + 1) * chunk, :]
            scores = jnp.dot(code_rows, encoded_ref[...], preferred_element_type=jnp.float32)
            logits = (scores * LOG2E - half_squares(code_rows)).reshape(chunk // 8, 8, rows)
            new_max = jnp.maximum(run_max, jnp.max(logits, axis=0))
            powers = jnp.exp2(logits - new_max[None])
            run_sum = run_sum * jnp.exp2(run_max - new_max) + jnp.sum(powers, axis=0)
            run_max = new_max
        top[...] = run_max
        total[...] = run_sum

        @pl.when(step == pl.num_programs(0) - 1)
        def _():
            row_max = jnp.max(run_max, axis=0, keepdims=True)
            max_ref[...] = row_max
            sum_ref[...] = jnp.sum(run_sum * jnp.exp2(run_max - row_max), axis=0, keepdims=True)

    out = jax.ShapeDtypeStruct((1, rows), jnp.float32)
    return pl.pallas_call(
        kernel,
        grid=(codes // block,),
        in_specs=[
            pl.BlockSpec((features, rows), lambda i: (0, 0)),
            pl.BlockSpec((block, features), lambda i: (i, 0)),
        ],
        out_specs=[pl.BlockSpec((1, rows), lambda i: (0, 0))] * 2,
        out_shape=[out, out],
        scratch_shapes=[pltpu.VMEM((8, rows), jnp.float32)] * 2,
        compiler_params=PARAMS,
        name="row_stats",
    )(encoded_t, codebook)


def place_of(offset, count):
    bits = count.bit_length() - 1
    return sum(((offset >> b) & 1) << (bits - 1 - b) for b in range(bits))


def mass_call(me, batch_rows, codebook, all_lse, devices, own):
    total_rows, features = batch_rows.shape
    rows = total_rows // devices
    block = math.gcd(own, 256)
    blocks = own // block

    def kernel(me_ref, rows_ref, codes_ref, lse_ref, log_ref, cross_ref, logits_scr):
        step = pl.program_id(0)

        @pl.when(step == 0)
        def _():
            cross_ref[...] = jnp.zeros(cross_ref.shape, jnp.float32)

        code_rows = codes_ref[...]
        squares = half_squares(code_rows)
        mass = jnp.zeros((block, rows), jnp.float32)
        for d in range(devices):
            part = slice(d * rows, (d + 1) * rows)
            scores = lax.dot_general(code_rows, rows_ref[part, :], NT, preferred_element_type=jnp.float32)
            place = place_of(me_ref[0] ^ d, devices)
            logits = scores * LOG2E - squares - lse_ref[pl.ds(place, 1), :]
            weights = jnp.exp2(logits)
            mass = mass + weights
            logits_scr[:, part] = logits
        log_mass = jnp.log2(jnp.sum(mass, axis=1, keepdims=True) * (1.0 / (LN2 * total_rows)))
        log_ref[...] = column_to_row(log_mass)
        for d in range(devices):
            part = slice(d * rows, (d + 1) * rows)
            logits = logits_scr[:, part]
            terms = jnp.exp2(logits) * (log_mass - logits)
            cross_ref[:, part] += jnp.sum(terms.reshape(block // 8, 8, rows), axis=0)

    return pl.pallas_call(
        kernel,
        grid_spec=pltpu.PrefetchScalarGridSpec(
            num_scalar_prefetch=1,
            grid=(blocks,),
            in_specs=[
                pl.BlockSpec((total_rows, features), lambda i, me: (0, 0)),
                pl.BlockSpec((block, features), lambda i, me: (me[0] * blocks + i, 0)),
                pl.BlockSpec((devices, rows), lambda i, me: (0, 0)),
            ],
            out_specs=[
                pl.BlockSpec((1, block), lambda i, me: (0, i)),
                pl.BlockSpec((8, total_rows), lambda i, me: (0, 0)),
            ],
            scratch_shapes=[pltpu.VMEM((block, total_rows), jnp.float32)],
        ),
        out_shape=[
            jax.ShapeDtypeStruct((1, own), jnp.float32),
            jax.ShapeDtypeStruct((8, total_rows), jnp.float32),
        ],
        compiler_params=PARAMS,
        name="code_mass",
    )(me, batch_rows, codebook, all_lse)


def rows_call(me, encoded, codebook, lse_wide, shift_wide, all_squares, all_log, devices, own):
    rows, features = encoded.shape
    codes = codebook.shape[0]
    block = math.gcd(own, 4096)
    per_device = own // block
    chunk = math.gcd(block, 512)

    def kernel(me_ref, encoded_ref, codes_ref, lse_ref, shift_ref, squares_ref, log_ref, out_ref):
        @pl.when(pl.program_id(0) == 0)
        def _():
            out_ref[...] = jnp.zeros(out_ref.shape, jnp.float32)

        encoded_here = encoded_ref[...]
        total = out_ref[...]
        for k in range(block // chunk):
            part = slice(k * chunk, (k + 1) * chunk)
            code_rows = codes_ref[part, :]
            scores = lax.dot_general(encoded_here, code_rows, NT, preferred_element_type=jnp.float32)
            squares = squares_ref[0, :, part]
            log_mass = log_ref[0, :, part]
            tiles = []
            for q in range(chunk // LANES):
                lane = slice(q * LANES, (q + 1) * LANES)
                logits = scores[:, lane] * LOG2E - squares[:, lane] - lse_ref[...]
                tile = jnp.exp2(logits) * (log_mass[:, lane] - logits + shift_ref[...])
                tiles.append(tile.astype(jnp.bfloat16))
            grad_tile = jnp.concatenate(tiles, axis=1)
            total = total + jnp.dot(grad_tile, code_rows, preferred_element_type=jnp.float32)
        out_ref[...] = total

    def vector_map(i, me):
        return (place_of(me[0] ^ (i // per_device), devices), 0, i % per_device)

    return pl.pallas_call(
        kernel,
        grid_spec=pltpu.PrefetchScalarGridSpec(
            num_scalar_prefetch=1,
            grid=(codes // block,),
            in_specs=[
                pl.BlockSpec((rows, features), lambda i, me: (0, 0)),
                pl.BlockSpec((block, features), lambda i, me: (i, 0)),
                pl.BlockSpec((rows, LANES), lambda i, me: (0, 0)),
                pl.BlockSpec((rows, LANES), lambda i, me: (0, 0)),
                pl.BlockSpec((1, 1, block), vector_map),
                pl.BlockSpec((1, 1, block), vector_map),
            ],
            out_specs=pl.BlockSpec((rows, features), lambda i, me: (0, 0)),
        ),
        out_shape=jax.ShapeDtypeStruct((rows, features), jnp.float32),
        compiler_params=PARAMS,
        name="grad_rows",
    )(me, encoded, codebook, lse_wide, shift_wide, all_squares, all_log)


def codes_call(me, batch_rows, codebook, all_lse, shift, log_mass, devices, own):
    total_rows, features = batch_rows.shape
    rows = total_rows // devices
    block = math.gcd(own, 512)
    blocks = own // block

    def kernel(me_ref, rows_ref, codes_ref, lse_ref, shift_ref, log_ref, out_ref):
        log_mass = jnp.transpose(jnp.broadcast_to(log_ref[...], (LANES, block)))[:, 0:1]
        code_rows = codes_ref[...]
        squares = half_squares(code_rows)
        total = jnp.zeros((block, features), jnp.float32)
        sums = jnp.zeros((block, rows), jnp.float32)
        for d in range(devices):
            part = slice(d * rows, (d + 1) * rows)
            row_block = rows_ref[part, :]
            scores = lax.dot_general(code_rows, row_block, NT, preferred_element_type=jnp.float32)
            place = place_of(me_ref[0] ^ d, devices)
            logits = scores * LOG2E - squares - lse_ref[pl.ds(place, 1), :]
            tile = jnp.exp2(logits) * (log_mass - logits + shift_ref[:, part])
            sums = sums + tile
            total = total + jnp.dot(
                tile.astype(jnp.bfloat16), row_block, preferred_element_type=jnp.float32
            )
        code_sums = jnp.sum(sums, axis=1, keepdims=True)
        out_ref[...] = total - code_sums * code_rows.astype(jnp.float32)

    return pl.pallas_call(
        kernel,
        grid_spec=pltpu.PrefetchScalarGridSpec(
            num_scalar_prefetch=1,
            grid=(blocks,),
            in_specs=[
                pl.BlockSpec((total_rows, features), lambda i, me: (0, 0)),
                pl.BlockSpec((block, features), lambda i, me: (me[0] * blocks + i, 0)),
                pl.BlockSpec((devices, rows), lambda i, me: (0, 0)),
                pl.BlockSpec((1, total_rows), lambda i, me: (0, 0)),
                pl.BlockSpec((1, block), lambda i, me: (0, i)),
            ],
            out_specs=pl.BlockSpec((block, features), lambda i, me: (i, 0)),
        ),
        out_shape=jax.ShapeDtypeStruct((own, features), jnp.float32),
        compiler_params=PARAMS,
        name="grad_codes",
    )(me, batch_rows, codebook, all_lse, shift, log_mass)


def from_xor(values, axis, offset):
    return lax.ppermute(values, axis, [(i, i ^ offset) for i in range(lax.axis_size(axis))])


def xor_gather(values, axis):
    held = values[None]
    offset = lax.axis_size(axis) // 2
    while offset:
        held = jnp.concatenate([held, from_xor(held, axis, offset)], axis=0)
        offset //= 2
    return held


def xor_sum(values, axis):
    offset = lax.axis_size(axis) // 2
    while offset:
        values = values + from_xor(values, axis, offset)
        offset //= 2
    return values


def body(encoded, codebook):
    rows, features = encoded.shape
    codes = codebook.shape[0]
    devices = lax.axis_size("dp")
    own = codes // devices
    me_index = lax.axis_index("dp")
    me = me_index.astype(jnp.int32).reshape(1)

    batch_rows = lax.all_gather(encoded, "dp", axis=0, tiled=True)
    own_codes = lax.dynamic_slice_in_dim(codebook, me_index * own, own, 0).astype(jnp.float32)
    own_squares = jnp.sum(own_codes * own_codes, axis=1) * (0.5 * LOG2E)

    row_max, row_sum = stats_call(encoded.T, codebook)
    stats = jnp.concatenate([row_max, row_sum], axis=0)
    offset = lax.axis_size("code") // 2
    while offset:
        other = from_xor(stats, "code", offset)
        top = jnp.maximum(stats[0:1], other[0:1])
        total = stats[1:2] * jnp.exp2(stats[0:1] - top) + other[1:2] * jnp.exp2(other[0:1] - top)
        stats = jnp.concatenate([top, total], axis=0)
        offset //= 2
    row_lse = (stats[0] + jnp.log2(stats[1])) - LOG2LN2

    gathered = xor_gather(jnp.concatenate([row_lse, own_squares]), "dp")
    all_lse, all_squares = gathered[:, :rows], gathered[:, None, rows:]

    log_mass, cross = mass_call(me, batch_rows, codebook, all_lse, devices, own)
    cross = xor_sum(jnp.sum(cross, axis=0), "code")
    gathered = xor_gather(jnp.concatenate([log_mass[0], cross]), "dp")
    all_log = gathered[:, None, :own]
    shift = jnp.sum(gathered[:, own:], axis=0) * (-1.0 / LN2)
    own_shift = lax.dynamic_slice_in_dim(shift, me_index * rows, rows, 0)

    local_rows = rows_call(
        me,
        encoded,
        codebook,
        jnp.broadcast_to(row_lse[:, None], (rows, LANES)),
        jnp.broadcast_to(own_shift[:, None], (rows, LANES)),
        all_squares,
        all_log,
        devices,
        own,
    )
    grad_codes = codes_call(me, batch_rows, codebook, all_lse, shift[None, :], log_mass, devices, own)
    grad_rows = xor_sum(local_rows, "code")
    return grad_rows, grad_codes


def solution(mesh):
    placed = (P("dp", None), P("code", None))
    return jax.shard_map(
        body,
        mesh=mesh,
        in_specs=placed,
        out_specs=(P("dp", None), P(("code", "dp"), None)),
        check_vma=False,
    )
```

```python
import math

import jax
import jax.numpy as jnp
from jax import lax
from jax.experimental import pallas as pl
from jax.experimental.pallas import tpu as pltpu
from jax.sharding import PartitionSpec as P

LOG2E = math.log2(math.e)
LN2 = math.log(2.0)
LOG2LN2 = math.log2(LN2)
LANES = 128
PARAMS = pltpu.CompilerParams(vmem_limit_bytes=56 * 2**20)
NT = (((1,), (1,)), ((), ()))


def squared(code_rows):
    values = code_rows.astype(jnp.float32)
    return jnp.sum(values * values, axis=1, keepdims=True)


def column_to_row(column):
    wide = jnp.broadcast_to(column, (column.shape[0], LANES))
    return jnp.transpose(wide)[0:1, :]


def row_to_columns(row):
    return jnp.transpose(jnp.broadcast_to(row, (LANES, row.shape[1])))


def stats_call(encoded, codebook, state, first, last):
    rows, features = encoded.shape
    block = math.gcd(math.gcd(first, last), 8192)
    chunk = math.gcd(block, 256)
    done = last == codebook.shape[0]

    def kernel(encoded_ref, codes_ref, state_ref, out_ref, turned, top, total):
        step = pl.program_id(0)

        @pl.when(step == 0)
        def _():
            turned[...] = jnp.transpose(encoded_ref[...]) * jnp.bfloat16(2.0)
            top[...] = state_ref[0]
            total[...] = state_ref[1]

        run_max, run_sum = top[...], total[...]
        for k in range(block // chunk):
            code_rows = codes_ref[k * chunk : (k + 1) * chunk, :]
            scores = jnp.dot(code_rows, turned[...], preferred_element_type=jnp.float32)
            logits = ((scores - squared(code_rows)) * (0.5 * LOG2E)).reshape(chunk // 8, 8, rows)
            new_max = jnp.maximum(run_max, jnp.max(logits, axis=0))
            powers = jnp.exp2(logits - new_max[None])
            run_sum = run_sum * jnp.exp2(run_max - new_max) + jnp.sum(powers, axis=0)
            run_max = new_max
        top[...] = run_max
        total[...] = run_sum

        @pl.when(step == pl.num_programs(0) - 1)
        def _():
            if done:
                row_max = jnp.max(run_max, axis=0, keepdims=True)
                out_ref[0:1, :] = row_max
                out_ref[1:2, :] = jnp.sum(run_sum * jnp.exp2(run_max - row_max), axis=0, keepdims=True)
            else:
                out_ref[0] = run_max
                out_ref[1] = run_sum

    shape = (2, rows) if done else (2, 8, rows)
    return pl.pallas_call(
        kernel,
        grid=((last - first) // block,),
        in_specs=[
            pl.BlockSpec((rows, features), lambda i: (0, 0)),
            pl.BlockSpec((block, features), lambda i: (first // block + i, 0)),
            pl.BlockSpec((2, 8, rows), lambda i: (0, 0, 0)),
        ],
        out_specs=pl.BlockSpec(shape, lambda i: (0,) * len(shape)),
        out_shape=jax.ShapeDtypeStruct(shape, jnp.float32),
        scratch_shapes=[pltpu.VMEM((features, rows), jnp.bfloat16)] + [pltpu.VMEM((8, rows), jnp.float32)] * 2,
        compiler_params=PARAMS,
        name="row_stats",
    )(encoded, codebook, state)


def place_of(offset, count):
    bits = count.bit_length() - 1
    return sum(((offset >> b) & 1) << (bits - 1 - b) for b in range(bits))


def piece_of(place, rows):
    piece = place.bit_length()
    return piece, (place - (1 << (piece - 1) if piece else 0)) * rows


def mass_call(me, pieces, codebook, all_lse, devices, own):
    rows, features = pieces[0].shape
    total_rows = rows * devices
    block = math.gcd(own, 512)
    steps = own // block

    def kernel(me_ref, codes_ref, lse_ref, *refs):
        row_refs, (log_ref, squares_ref, cross_ref, cross, logits_scr) = refs[: len(pieces)], refs[len(pieces) :]
        step = pl.program_id(0)

        @pl.when(step == 0)
        def _():
            cross[...] = jnp.zeros(cross.shape, jnp.float32)

        code_rows = codes_ref[...]
        squares = squared(code_rows)
        half = jnp.broadcast_to(squares, (block, LANES))
        doubled = code_rows * jnp.bfloat16(2.0)
        mass = jnp.zeros((block, LANES), jnp.float32)
        for p in range(devices):
            piece, start = piece_of(p, rows)
            row_block = row_refs[piece][start : start + rows, :]
            scores = lax.dot_general(doubled, row_block, NT, preferred_element_type=jnp.float32)
            for q in range(rows // LANES):
                lane = slice(q * LANES, (q + 1) * LANES)
                logits = (scores[:, lane] - half) * (0.5 * LOG2E) - lse_ref[p, :, lane]
                logits_scr[:, p * rows + q * LANES : p * rows + (q + 1) * LANES] = logits
                mass = mass + jnp.exp2(logits)
        log_mass = jnp.log2(jnp.sum(mass, axis=1, keepdims=True) * (1.0 / (LN2 * total_rows)))
        log_ref[0] = column_to_row(log_mass)
        squares_ref[0] = column_to_row(squares) * (0.5 * LOG2E)
        log_wide = jnp.broadcast_to(log_mass, (block, LANES))
        for q in range(total_rows // LANES):
            there = slice(q * LANES, (q + 1) * LANES)
            logits = logits_scr[:, there]
            terms = jnp.exp2(logits) * (log_wide - logits)
            cross[:, there] += jnp.sum(terms.reshape(block // 8, 8, LANES), axis=0)

        @pl.when(step == pl.num_programs(0) - 1)
        def _():
            for p in range(devices):
                there = pl.ds(pl.multiple_of((me_ref[0] ^ place_of(p, devices)) * rows, rows), rows)
                cross_ref[:, there] = jnp.sum(cross[:, p * rows : (p + 1) * rows], axis=0, keepdims=True)

    return pl.pallas_call(
        kernel,
        grid_spec=pltpu.PrefetchScalarGridSpec(
            num_scalar_prefetch=1,
            grid=(steps,),
            in_specs=[
                pl.BlockSpec((block, features), lambda i, me: (me[0] * steps + i, 0)),
                pl.BlockSpec((devices, 1, rows), lambda i, me: (0, 0, 0)),
            ]
            + [pl.BlockSpec(piece.shape, lambda i, me: (0, 0)) for piece in pieces],
            out_specs=[
                pl.BlockSpec((1, 1, block), lambda i, me: (0, 0, i)),
                pl.BlockSpec((1, 1, block), lambda i, me: (0, 0, i)),
                pl.BlockSpec((1, total_rows), lambda i, me: (0, 0)),
            ],
            scratch_shapes=[
                pltpu.VMEM((8, total_rows), jnp.float32),
                pltpu.VMEM((block, total_rows), jnp.float32),
            ],
        ),
        out_shape=[
            jax.ShapeDtypeStruct((1, 1, own), jnp.float32),
            jax.ShapeDtypeStruct((1, 1, own), jnp.float32),
            jax.ShapeDtypeStruct((1, total_rows), jnp.float32),
        ],
        compiler_params=PARAMS,
        name="code_mass",
    )(me, codebook, all_lse, *pieces)


def rows_call(me, encoded, codebook, row_lse, shift, gathered, devices, own):
    rows, features = encoded.shape
    codes = codebook.shape[0]
    block = math.gcd(own, 4096)
    per_device = own // block
    chunk = math.gcd(block, 512)

    def kernel(me_ref, encoded_ref, codes_ref, lse_ref, shift_ref, log_ref, squares_ref, out_ref, lse_wide, shift_wide):
        @pl.when(pl.program_id(0) == 0)
        def _():
            out_ref[...] = jnp.zeros(out_ref.shape, jnp.float32)
            mine = pl.ds(pl.multiple_of(me_ref[0] * rows, rows), rows)
            lse_wide[...] = row_to_columns(lse_ref[...])
            shift_wide[...] = row_to_columns(shift_ref[:, mine])

        encoded_here = encoded_ref[...]
        total = out_ref[...]
        for k in range(block // chunk):
            part = slice(k * chunk, (k + 1) * chunk)
            code_rows = codes_ref[part, :]
            scores = lax.dot_general(encoded_here, code_rows, NT, preferred_element_type=jnp.float32)
            log_mass = log_ref[0, :, part]
            squares = squares_ref[0, :, part]
            tiles = []
            for q in range(chunk // LANES):
                lane = slice(q * LANES, (q + 1) * LANES)
                logits = scores[:, lane] * LOG2E - squares[:, lane] - lse_wide[...]
                tile = jnp.exp2(logits) * (log_mass[:, lane] - logits + shift_wide[...])
                tiles.append(tile.astype(jnp.bfloat16))
            grad_tile = jnp.concatenate(tiles, axis=1)
            total = total + jnp.dot(grad_tile, code_rows, preferred_element_type=jnp.float32)
        out_ref[...] = total

    def log_map(i, me):
        return (place_of(me[0] ^ (i // per_device), devices), 0, i % per_device)

    def squares_map(i, me):
        return (place_of(me[0] ^ (i // per_device), devices), 0, per_device + i % per_device)

    return pl.pallas_call(
        kernel,
        grid_spec=pltpu.PrefetchScalarGridSpec(
            num_scalar_prefetch=1,
            grid=(codes // block,),
            in_specs=[
                pl.BlockSpec((rows, features), lambda i, me: (0, 0)),
                pl.BlockSpec((block, features), lambda i, me: (i, 0)),
                pl.BlockSpec(row_lse.shape, lambda i, me: (0, 0)),
                pl.BlockSpec(shift.shape, lambda i, me: (0, 0)),
                pl.BlockSpec((1, 1, block), log_map),
                pl.BlockSpec((1, 1, block), squares_map),
            ],
            out_specs=pl.BlockSpec((rows, features), lambda i, me: (0, 0)),
            scratch_shapes=[pltpu.VMEM((rows, LANES), jnp.float32)] * 2,
        ),
        out_shape=jax.ShapeDtypeStruct((rows, features), jnp.float32),
        compiler_params=PARAMS,
        name="grad_rows",
    )(me, encoded, codebook, row_lse, shift, gathered, gathered)


def codes_call(me, pieces, codebook, all_lse, shift, log_mass, squares, devices, own, CHAINS=1, BLOCK=512):
    rows, features = pieces[0].shape
    block = math.gcd(own, BLOCK)
    blocks = own // block

    def kernel(me_ref, codes_ref, lse_ref, shift_ref, log_ref, squares_ref, *refs):
        row_refs, out_ref = refs[:-1], refs[-1]
        log_mass = row_to_columns(log_ref[0])
        half = row_to_columns(squares_ref[0])
        code_rows = codes_ref[...]
        totals = [jnp.zeros((block, features), jnp.float32)] * CHAINS
        sums = jnp.zeros((block, LANES), jnp.float32)
        for p in range(devices):
            piece, start = piece_of(p, rows)
            row_block = row_refs[piece][start : start + rows, :]
            scores = lax.dot_general(code_rows, row_block, NT, preferred_element_type=jnp.float32)
            there = pl.ds(pl.multiple_of((me_ref[0] ^ place_of(p, devices)) * rows, rows), rows)
            shift_here = shift_ref[:, there]
            tiles = []
            for q in range(rows // LANES):
                lane = slice(q * LANES, (q + 1) * LANES)
                logits = scores[:, lane] * LOG2E - half - lse_ref[p, :, lane]
                tile = jnp.exp2(logits) * (log_mass - logits + shift_here[:, lane])
                sums = sums + tile
                tiles.append(tile.astype(jnp.bfloat16))
            grad_tile = jnp.concatenate(tiles, axis=1)
            totals[p % CHAINS] = totals[p % CHAINS] + jnp.dot(
                grad_tile, row_block, preferred_element_type=jnp.float32
            )
        code_sums = jnp.sum(sums, axis=1, keepdims=True)
        out_ref[...] = sum(totals) - code_sums * code_rows.astype(jnp.float32)

    return pl.pallas_call(
        kernel,
        grid_spec=pltpu.PrefetchScalarGridSpec(
            num_scalar_prefetch=1,
            grid=(blocks,),
            in_specs=[
                pl.BlockSpec((block, features), lambda i, me: (me[0] * blocks + i, 0)),
                pl.BlockSpec((devices, 1, rows), lambda i, me: (0, 0, 0)),
                pl.BlockSpec((1, rows * devices), lambda i, me: (0, 0)),
                pl.BlockSpec((1, 1, block), lambda i, me: (0, 0, i)),
                pl.BlockSpec((1, 1, block), lambda i, me: (0, 0, i)),
            ]
            + [pl.BlockSpec(piece.shape, lambda i, me: (0, 0)) for piece in pieces],
            out_specs=pl.BlockSpec((block, features), lambda i, me: (i, 0)),
        ),
        out_shape=jax.ShapeDtypeStruct((own, features), jnp.float32),
        compiler_params=PARAMS,
        name="grad_codes",
    )(me, codebook, all_lse, shift, log_mass, squares, *pieces)


def from_xor(values, axis, offset):
    return lax.ppermute(values, axis, [(i, i ^ offset) for i in range(lax.axis_size(axis))])


def xor_gather(held, axis):
    offset = lax.axis_size(axis) // 2
    while offset:
        held = jnp.concatenate([held, from_xor(held, axis, offset)], axis=0)
        offset //= 2
    return held


def xor_sum(values, axis):
    offset = lax.axis_size(axis) // 2
    while offset:
        values = values + from_xor(values, axis, offset)
        offset //= 2
    return values


def body(encoded, codebook):
    rows, features = encoded.shape
    codes = codebook.shape[0]
    devices = lax.axis_size("dp")
    own = codes // devices
    me = lax.axis_index("dp").astype(jnp.int32).reshape(1)
    offsets = [devices >> (k + 1) for k in range(devices.bit_length() - 1)]

    pieces = [encoded]

    def gather_more(after):
        if len(pieces) > len(offsets):
            return after
        held, after = lax.optimization_barrier((tuple(pieces), after))
        pieces[:] = held
        joined = lax.optimization_barrier(jnp.concatenate(pieces, axis=0)) if len(pieces) > 1 else encoded
        pieces.append(from_xor(joined, "dp", offsets[len(pieces) - 1]))
        return after

    state = jnp.stack([jnp.full((8, rows), -3e38, jnp.float32), jnp.zeros((8, rows), jnp.float32)])
    state = gather_more(state)
    state = stats_call(encoded, codebook, state, 0, codes // 2)
    state = gather_more(state)
    stats = stats_call(encoded, codebook, state, codes // 2, codes)
    stats = gather_more(stats)
    offset = lax.axis_size("code") // 2
    while offset:
        other = from_xor(stats, "code", offset)
        top = jnp.maximum(stats[0:1], other[0:1])
        total = stats[1:2] * jnp.exp2(stats[0:1] - top) + other[1:2] * jnp.exp2(other[0:1] - top)
        stats = jnp.concatenate([top, total], axis=0)
        offset //= 2
    row_lse = stats[0:1] + jnp.log2(stats[1:2]) - LOG2LN2
    all_lse = lax.optimization_barrier(row_lse[None])
    for k, offset in enumerate(offsets):
        all_lse = jnp.concatenate([all_lse, from_xor(all_lse, "dp", offset)], axis=0)
        if k:
            all_lse = gather_more(all_lse)

    log_mass, squares, cross = mass_call(me, pieces, codebook, all_lse, devices, own)
    cross = xor_sum(cross, "code")
    message = jnp.concatenate([log_mass, squares, cross[None]], axis=2)
    gathered = xor_gather(lax.optimization_barrier(message), "dp")
    shift = jnp.sum(gathered[:, :, 2 * own :], axis=0) * (-1.0 / LN2)

    local_rows = rows_call(me, encoded, codebook, row_lse, shift, gathered, devices, own)
    grad_codes = codes_call(me, pieces, codebook, all_lse, shift, log_mass, squares, devices, own)
    grad_rows = xor_sum(local_rows, "code")
    return grad_rows, grad_codes


def solution(mesh):
    placed = (P("dp", None), P("code", None))
    return jax.shard_map(
        body,
        mesh=mesh,
        in_specs=placed,
        out_specs=(P("dp", None), P(("code", "dp"), None)),
        check_vma=False,
    )
```

```python
import math

import jax
import jax.numpy as jnp
from jax import lax
from jax.experimental import pallas as pl
from jax.experimental.pallas import tpu as pltpu
from jax.sharding import PartitionSpec as P

LOG2E = math.log2(math.e)
LN2 = math.log(2.0)
LOG2LN2 = math.log2(LN2)
LANES = 128
PARAMS = pltpu.CompilerParams(vmem_limit_bytes=56 * 2**20)
NT = (((1,), (1,)), ((), ()))


def squared(code_rows):
    values = code_rows.astype(jnp.float32)
    return jnp.sum(values * values, axis=1, keepdims=True)


def column_to_row(column):
    wide = jnp.broadcast_to(column, (column.shape[0], LANES))
    return jnp.transpose(wide)[0:1, :]


def row_to_columns(row):
    return jnp.transpose(jnp.broadcast_to(row, (LANES, row.shape[1])))


def stats_call(encoded, codebook, state, first, last):
    rows, features = encoded.shape
    block = math.gcd(math.gcd(first, last), 8192)
    chunk = math.gcd(block, 256)
    done = last == codebook.shape[0]

    def kernel(encoded_ref, codes_ref, state_ref, out_ref, turned, top, total):
        step = pl.program_id(0)

        @pl.when(step == 0)
        def _():
            turned[...] = jnp.transpose(encoded_ref[...]) * jnp.bfloat16(2.0)
            top[...] = state_ref[0]
            total[...] = state_ref[1]

        run_max, run_sum = top[...], total[...]
        for k in range(block // chunk):
            code_rows = codes_ref[k * chunk : (k + 1) * chunk, :]
            scores = jnp.dot(code_rows, turned[...], preferred_element_type=jnp.float32)
            logits = ((scores - squared(code_rows)) * (0.5 * LOG2E)).reshape(chunk // 8, 8, rows)
            new_max = jnp.maximum(run_max, jnp.max(logits, axis=0))
            powers = jnp.exp2(logits - new_max[None])
            run_sum = run_sum * jnp.exp2(run_max - new_max) + jnp.sum(powers, axis=0)
            run_max = new_max
        top[...] = run_max
        total[...] = run_sum

        @pl.when(step == pl.num_programs(0) - 1)
        def _():
            if done:
                row_max = jnp.max(run_max, axis=0, keepdims=True)
                out_ref[0:1, :] = row_max
                out_ref[1:2, :] = jnp.sum(run_sum * jnp.exp2(run_max - row_max), axis=0, keepdims=True)
            else:
                out_ref[0] = run_max
                out_ref[1] = run_sum

    shape = (2, rows) if done else (2, 8, rows)
    return pl.pallas_call(
        kernel,
        grid=((last - first) // block,),
        in_specs=[
            pl.BlockSpec((rows, features), lambda i: (0, 0)),
            pl.BlockSpec((block, features), lambda i: (first // block + i, 0)),
            pl.BlockSpec((2, 8, rows), lambda i: (0, 0, 0)),
        ],
        out_specs=pl.BlockSpec(shape, lambda i: (0,) * len(shape)),
        out_shape=jax.ShapeDtypeStruct(shape, jnp.float32),
        scratch_shapes=[pltpu.VMEM((features, rows), jnp.bfloat16)] + [pltpu.VMEM((8, rows), jnp.float32)] * 2,
        compiler_params=PARAMS,
        name="row_stats",
    )(encoded, codebook, state)


def place_of(offset, count):
    bits = count.bit_length() - 1
    return sum(((offset >> b) & 1) << (bits - 1 - b) for b in range(bits))


def piece_of(place, rows):
    piece = place.bit_length()
    return piece, (place - (1 << (piece - 1) if piece else 0)) * rows


def mass_call(me, pieces, codebook, all_lse, devices, own):
    rows, features = pieces[0].shape
    total_rows = rows * devices
    block = math.gcd(own, 512)
    steps = own // block

    def kernel(me_ref, codes_ref, lse_ref, *refs):
        row_refs, (log_ref, squares_ref, cross_ref, cross, logits_scr) = refs[: len(pieces)], refs[len(pieces) :]
        step = pl.program_id(0)

        @pl.when(step == 0)
        def _():
            cross[...] = jnp.zeros(cross.shape, jnp.float32)

        code_rows = codes_ref[...]
        squares = squared(code_rows)
        half = jnp.broadcast_to(squares, (block, LANES))
        doubled = code_rows * jnp.bfloat16(2.0)
        mass = jnp.zeros((block, LANES), jnp.float32)
        for p in range(devices):
            piece, start = piece_of(p, rows)
            row_block = row_refs[piece][start : start + rows, :]
            scores = lax.dot_general(doubled, row_block, NT, preferred_element_type=jnp.float32)
            for q in range(rows // LANES):
                lane = slice(q * LANES, (q + 1) * LANES)
                logits = (scores[:, lane] - half) * (0.5 * LOG2E) - lse_ref[p, :, lane]
                logits_scr[:, p * rows + q * LANES : p * rows + (q + 1) * LANES] = logits
                mass = mass + jnp.exp2(logits)
        log_mass = jnp.log2(jnp.sum(mass, axis=1, keepdims=True) * (1.0 / (LN2 * total_rows)))
        log_ref[0] = column_to_row(log_mass)
        squares_ref[0] = column_to_row(squares) * (0.5 * LOG2E)
        log_wide = jnp.broadcast_to(log_mass, (block, LANES))
        for q in range(total_rows // LANES):
            there = slice(q * LANES, (q + 1) * LANES)
            logits = logits_scr[:, there]
            terms = jnp.exp2(logits) * (log_wide - logits)
            cross[:, there] += jnp.sum(terms.reshape(block // 8, 8, LANES), axis=0)

        @pl.when(step == pl.num_programs(0) - 1)
        def _():
            for p in range(devices):
                there = pl.ds(pl.multiple_of((me_ref[0] ^ place_of(p, devices)) * rows, rows), rows)
                cross_ref[:, there] = jnp.sum(cross[:, p * rows : (p + 1) * rows], axis=0, keepdims=True)

    return pl.pallas_call(
        kernel,
        grid_spec=pltpu.PrefetchScalarGridSpec(
            num_scalar_prefetch=1,
            grid=(steps,),
            in_specs=[
                pl.BlockSpec((block, features), lambda i, me: (me[0] * steps + i, 0)),
                pl.BlockSpec((devices, 1, rows), lambda i, me: (0, 0, 0)),
            ]
            + [pl.BlockSpec(piece.shape, lambda i, me: (0, 0)) for piece in pieces],
            out_specs=[
                pl.BlockSpec((1, 1, block), lambda i, me: (0, 0, i)),
                pl.BlockSpec((1, 1, block), lambda i, me: (0, 0, i)),
                pl.BlockSpec((1, total_rows), lambda i, me: (0, 0)),
            ],
            scratch_shapes=[
                pltpu.VMEM((8, total_rows), jnp.float32),
                pltpu.VMEM((block, total_rows), jnp.float32),
            ],
        ),
        out_shape=[
            jax.ShapeDtypeStruct((1, 1, own), jnp.float32),
            jax.ShapeDtypeStruct((1, 1, own), jnp.float32),
            jax.ShapeDtypeStruct((1, total_rows), jnp.float32),
        ],
        compiler_params=PARAMS,
        name="code_mass",
    )(me, codebook, all_lse, *pieces)


def rows_call(me, encoded, codebook, row_lse, shift, gathered, devices, own):
    rows, features = encoded.shape
    codes = codebook.shape[0]
    span = math.gcd(devices, max(1, 8192 // own))
    block = span * own
    chunk = math.gcd(own, 512)

    def kernel(me_ref, encoded_ref, codes_ref, lse_ref, shift_ref, vectors_ref, out_ref, lse_wide, shift_wide):
        step = pl.program_id(0)

        @pl.when(step == 0)
        def _():
            out_ref[...] = jnp.zeros(out_ref.shape, jnp.float32)
            mine = pl.ds(pl.multiple_of(me_ref[0] * rows, rows), rows)
            lse_wide[...] = row_to_columns(lse_ref[...])
            shift_wide[...] = row_to_columns(shift_ref[:, mine])

        encoded_here = encoded_ref[...]
        total = out_ref[...]
        for k in range(block // chunk):
            code_rows = codes_ref[k * chunk : (k + 1) * chunk, :]
            scores = lax.dot_general(encoded_here, code_rows, NT, preferred_element_type=jnp.float32)
            owner, start = divmod(k * chunk, own)
            place = place_of(me_ref[0] ^ (step * span + owner), devices)
            log_mass = vectors_ref[place, :, start : start + chunk]
            squares = vectors_ref[place, :, own + start : own + start + chunk]
            tiles = []
            for q in range(chunk // LANES):
                lane = slice(q * LANES, (q + 1) * LANES)
                logits = scores[:, lane] * LOG2E - squares[:, lane] - lse_wide[...]
                tile = jnp.exp2(logits) * (log_mass[:, lane] - logits + shift_wide[...])
                tiles.append(tile.astype(jnp.bfloat16))
            grad_tile = jnp.concatenate(tiles, axis=1)
            total = total + jnp.dot(grad_tile, code_rows, preferred_element_type=jnp.float32)
        out_ref[...] = total

    return pl.pallas_call(
        kernel,
        grid_spec=pltpu.PrefetchScalarGridSpec(
            num_scalar_prefetch=1,
            grid=(codes // block,),
            in_specs=[
                pl.BlockSpec((rows, features), lambda i, me: (0, 0)),
                pl.BlockSpec((block, features), lambda i, me: (i, 0)),
                pl.BlockSpec(row_lse.shape, lambda i, me: (0, 0)),
                pl.BlockSpec(shift.shape, lambda i, me: (0, 0)),
                pl.BlockSpec((devices, 1, 2 * own), lambda i, me: (0, 0, 0)),
            ],
            out_specs=pl.BlockSpec((rows, features), lambda i, me: (0, 0)),
            scratch_shapes=[pltpu.VMEM((rows, LANES), jnp.float32)] * 2,
        ),
        out_shape=jax.ShapeDtypeStruct((rows, features), jnp.float32),
        compiler_params=PARAMS,
        name="grad_rows",
    )(me, encoded, codebook, row_lse, shift, gathered)


def codes_call(me, pieces, codebook, all_lse, shift, log_mass, squares, devices, own):
    rows, features = pieces[0].shape
    block = math.gcd(own, 1024)
    blocks = own // block

    def kernel(me_ref, codes_ref, lse_ref, shift_ref, log_ref, squares_ref, *refs):
        row_refs, out_ref = refs[:-1], refs[-1]
        log_mass = row_to_columns(log_ref[0])
        half = row_to_columns(squares_ref[0])
        code_rows = codes_ref[...]
        total = jnp.zeros((block, features), jnp.float32)
        sums = jnp.zeros((block, LANES), jnp.float32)
        for p in range(devices):
            piece, start = piece_of(p, rows)
            row_block = row_refs[piece][start : start + rows, :]
            scores = lax.dot_general(code_rows, row_block, NT, preferred_element_type=jnp.float32)
            there = pl.ds(pl.multiple_of((me_ref[0] ^ place_of(p, devices)) * rows, rows), rows)
            shift_here = shift_ref[:, there]
            tiles = []
            for q in range(rows // LANES):
                lane = slice(q * LANES, (q + 1) * LANES)
                logits = scores[:, lane] * LOG2E - half - lse_ref[p, :, lane]
                tile = jnp.exp2(logits) * (log_mass - logits + shift_here[:, lane])
                sums = sums + tile
                tiles.append(tile.astype(jnp.bfloat16))
            grad_tile = jnp.concatenate(tiles, axis=1)
            total = total + jnp.dot(grad_tile, row_block, preferred_element_type=jnp.float32)
        code_sums = jnp.sum(sums, axis=1, keepdims=True)
        out_ref[...] = total - code_sums * code_rows.astype(jnp.float32)

    return pl.pallas_call(
        kernel,
        grid_spec=pltpu.PrefetchScalarGridSpec(
            num_scalar_prefetch=1,
            grid=(blocks,),
            in_specs=[
                pl.BlockSpec((block, features), lambda i, me: (me[0] * blocks + i, 0)),
                pl.BlockSpec((devices, 1, rows), lambda i, me: (0, 0, 0)),
                pl.BlockSpec((1, rows * devices), lambda i, me: (0, 0)),
                pl.BlockSpec((1, 1, block), lambda i, me: (0, 0, i)),
                pl.BlockSpec((1, 1, block), lambda i, me: (0, 0, i)),
            ]
            + [pl.BlockSpec(piece.shape, lambda i, me: (0, 0)) for piece in pieces],
            out_specs=pl.BlockSpec((block, features), lambda i, me: (i, 0)),
        ),
        out_shape=jax.ShapeDtypeStruct((own, features), jnp.float32),
        compiler_params=PARAMS,
        name="grad_codes",
    )(me, codebook, all_lse, shift, log_mass, squares, *pieces)


def from_xor(values, axis, offset):
    return lax.ppermute(values, axis, [(i, i ^ offset) for i in range(lax.axis_size(axis))])


def xor_gather(held, axis):
    offset = lax.axis_size(axis) // 2
    while offset:
        held = jnp.concatenate([held, from_xor(held, axis, offset)], axis=0)
        offset //= 2
    return held


def xor_sum(values, axis):
    offset = lax.axis_size(axis) // 2
    while offset:
        values = values + from_xor(values, axis, offset)
        offset //= 2
    return values


def body(encoded, codebook):
    rows, features = encoded.shape
    codes = codebook.shape[0]
    devices = lax.axis_size("dp")
    own = codes // devices
    me = lax.axis_index("dp").astype(jnp.int32).reshape(1)
    offsets = [devices >> (k + 1) for k in range(devices.bit_length() - 1)]

    pieces = [encoded]

    def gather_more(after):
        if len(pieces) > len(offsets):
            return after
        held, after = lax.optimization_barrier((tuple(pieces), after))
        pieces[:] = held
        joined = lax.optimization_barrier(jnp.concatenate(pieces, axis=0)) if len(pieces) > 1 else encoded
        pieces.append(from_xor(joined, "dp", offsets[len(pieces) - 1]))
        return after

    state = jnp.stack([jnp.full((8, rows), -3e38, jnp.float32), jnp.zeros((8, rows), jnp.float32)])
    state = gather_more(state)
    state = stats_call(encoded, codebook, state, 0, codes // 2)
    state = gather_more(state)
    stats = stats_call(encoded, codebook, state, codes // 2, codes)
    stats = gather_more(stats)
    offset = lax.axis_size("code") // 2
    while offset:
        other = from_xor(stats, "code", offset)
        top = jnp.maximum(stats[0:1], other[0:1])
        total = stats[1:2] * jnp.exp2(stats[0:1] - top) + other[1:2] * jnp.exp2(other[0:1] - top)
        stats = jnp.concatenate([top, total], axis=0)
        offset //= 2
    row_lse = stats[0:1] + jnp.log2(stats[1:2]) - LOG2LN2
    all_lse = lax.optimization_barrier(row_lse[None])
    for k, offset in enumerate(offsets):
        all_lse = jnp.concatenate([all_lse, from_xor(all_lse, "dp", offset)], axis=0)
        if k:
            all_lse = gather_more(all_lse)

    log_mass, squares, cross = mass_call(me, pieces, codebook, all_lse, devices, own)
    offset = lax.axis_size("code") // 2
    while offset > 1:
        cross = cross + from_xor(cross, "code", offset)
        offset //= 2
    message = jnp.concatenate([log_mass, squares, cross[None]], axis=2)
    if offset:
        message = message + jnp.pad(from_xor(cross, "code", offset)[None], ((0, 0), (0, 0), (2 * own, 0)))
    gathered = xor_gather(lax.optimization_barrier(message), "dp")
    shift = jnp.sum(gathered[:, :, 2 * own :], axis=0) * (-1.0 / LN2)

    local_rows = rows_call(me, encoded, codebook, row_lse, shift, gathered, devices, own)
    grad_codes = codes_call(me, pieces, codebook, all_lse, shift, log_mass, squares, devices, own)
    grad_rows = xor_sum(local_rows, "code")
    return grad_rows, grad_codes


def solution(mesh):
    placed = (P("dp", None), P("code", None))
    return jax.shard_map(
        body,
        mesh=mesh,
        in_specs=placed,
        out_specs=(P("dp", None), P(("code", "dp"), None)),
        check_vma=False,
    )
```

```python
import math

import jax
import jax.numpy as jnp
from jax import lax
from jax.experimental import pallas as pl
from jax.experimental.pallas import tpu as pltpu
from jax.sharding import PartitionSpec as P

LOG2E = math.log2(math.e)
LN2 = math.log(2.0)
LOG2LN2 = math.log2(LN2)
LANES = 128
PARAMS = pltpu.CompilerParams(vmem_limit_bytes=56 * 2**20)
NT = (((1,), (1,)), ((), ()))


def squared(code_rows):
    values = code_rows.astype(jnp.float32)
    return jnp.sum(values * values, axis=1, keepdims=True)


def column_to_row(column):
    wide = jnp.broadcast_to(column, (column.shape[0], LANES))
    return jnp.transpose(wide)[0:1, :]


def row_to_columns(row):
    return jnp.transpose(jnp.broadcast_to(row, (LANES, row.shape[1])))


def stats_call(encoded, codebook, state, first, last):
    rows, features = encoded.shape
    block = math.gcd(math.gcd(first, last), 8192)
    chunk = math.gcd(block, 256)
    done = last == codebook.shape[0]

    def kernel(encoded_ref, codes_ref, state_ref, out_ref, turned, top, total):
        step = pl.program_id(0)

        @pl.when(step == 0)
        def _():
            turned[...] = jnp.transpose(encoded_ref[...]) * jnp.bfloat16(2.0)
            top[...] = state_ref[0]
            total[...] = state_ref[1]

        run_max, run_sum = top[...], total[...]
        for k in range(block // chunk):
            code_rows = codes_ref[k * chunk : (k + 1) * chunk, :]
            scores = jnp.dot(code_rows, turned[...], preferred_element_type=jnp.float32)
            logits = ((scores - squared(code_rows)) * (0.5 * LOG2E)).reshape(chunk // 8, 8, rows)
            new_max = jnp.maximum(run_max, jnp.max(logits, axis=0))
            powers = jnp.exp2(logits - new_max[None])
            run_sum = run_sum * jnp.exp2(run_max - new_max) + jnp.sum(powers, axis=0)
            run_max = new_max
        top[...] = run_max
        total[...] = run_sum

        @pl.when(step == pl.num_programs(0) - 1)
        def _():
            if done:
                row_max = jnp.max(run_max, axis=0, keepdims=True)
                out_ref[0:1, :] = row_max
                out_ref[1:2, :] = jnp.sum(run_sum * jnp.exp2(run_max - row_max), axis=0, keepdims=True)
            else:
                out_ref[0] = run_max
                out_ref[1] = run_sum

    shape = (2, rows) if done else (2, 8, rows)
    return pl.pallas_call(
        kernel,
        grid=((last - first) // block,),
        in_specs=[
            pl.BlockSpec((rows, features), lambda i: (0, 0)),
            pl.BlockSpec((block, features), lambda i: (first // block + i, 0)),
            pl.BlockSpec((2, 8, rows), lambda i: (0, 0, 0)),
        ],
        out_specs=pl.BlockSpec(shape, lambda i: (0,) * len(shape)),
        out_shape=jax.ShapeDtypeStruct(shape, jnp.float32),
        scratch_shapes=[pltpu.VMEM((features, rows), jnp.bfloat16)] + [pltpu.VMEM((8, rows), jnp.float32)] * 2,
        compiler_params=PARAMS,
        name="row_stats",
    )(encoded, codebook, state)


def place_of(offset, count):
    bits = count.bit_length() - 1
    return sum(((offset >> b) & 1) << (bits - 1 - b) for b in range(bits))


def piece_of(place, rows):
    piece = place.bit_length()
    return piece, (place - (1 << (piece - 1) if piece else 0)) * rows


def mass_call(me, pieces, codebook, all_lse, devices, own):
    rows, features = pieces[0].shape
    total_rows = rows * devices
    block = math.gcd(own, 1024)
    steps = own // block

    def kernel(me_ref, codes_ref, lse_ref, *refs):
        row_refs, (log_ref, squares_ref, cross_ref, cross, logits_scr) = refs[: len(pieces)], refs[len(pieces) :]
        step = pl.program_id(0)

        @pl.when(step == 0)
        def _():
            cross[...] = jnp.zeros(cross.shape, jnp.float32)

        code_rows = codes_ref[...]
        squares = squared(code_rows)
        half = jnp.broadcast_to(squares, (block, LANES))
        doubled = code_rows * jnp.bfloat16(2.0)
        mass = jnp.zeros((block, LANES), jnp.float32)
        for p in range(devices):
            piece, start = piece_of(p, rows)
            row_block = row_refs[piece][start : start + rows, :]
            scores = lax.dot_general(doubled, row_block, NT, preferred_element_type=jnp.float32)
            for q in range(rows // LANES):
                lane = slice(q * LANES, (q + 1) * LANES)
                logits = (scores[:, lane] - half) * (0.5 * LOG2E) - lse_ref[p, :, lane]
                logits_scr[:, p * rows + q * LANES : p * rows + (q + 1) * LANES] = logits
                mass = mass + jnp.exp2(logits)
        log_mass = jnp.log2(jnp.sum(mass, axis=1, keepdims=True) * (1.0 / (LN2 * total_rows)))
        log_ref[0] = column_to_row(log_mass)
        squares_ref[0] = column_to_row(squares) * (0.5 * LOG2E)
        log_wide = jnp.broadcast_to(log_mass, (block, LANES))
        for q in range(total_rows // LANES):
            there = slice(q * LANES, (q + 1) * LANES)
            logits = logits_scr[:, there]
            terms = jnp.exp2(logits) * (log_wide - logits)
            cross[:, there] += jnp.sum(terms.reshape(block // 8, 8, LANES), axis=0)

        @pl.when(step == pl.num_programs(0) - 1)
        def _():
            for p in range(devices):
                there = pl.ds(pl.multiple_of((me_ref[0] ^ place_of(p, devices)) * rows, rows), rows)
                cross_ref[:, there] = jnp.sum(cross[:, p * rows : (p + 1) * rows], axis=0, keepdims=True)

    return pl.pallas_call(
        kernel,
        grid_spec=pltpu.PrefetchScalarGridSpec(
            num_scalar_prefetch=1,
            grid=(steps,),
            in_specs=[
                pl.BlockSpec((block, features), lambda i, me: (me[0] * steps + i, 0)),
                pl.BlockSpec((devices, 1, rows), lambda i, me: (0, 0, 0)),
            ]
            + [pl.BlockSpec(piece.shape, lambda i, me: (0, 0)) for piece in pieces],
            out_specs=[
                pl.BlockSpec((1, 1, block), lambda i, me: (0, 0, i)),
                pl.BlockSpec((1, 1, block), lambda i, me: (0, 0, i)),
                pl.BlockSpec((1, total_rows), lambda i, me: (0, 0)),
            ],
            scratch_shapes=[
                pltpu.VMEM((8, total_rows), jnp.float32),
                pltpu.VMEM((block, total_rows), jnp.float32),
            ],
        ),
        out_shape=[
            jax.ShapeDtypeStruct((1, 1, own), jnp.float32),
            jax.ShapeDtypeStruct((1, 1, own), jnp.float32),
            jax.ShapeDtypeStruct((1, total_rows), jnp.float32),
        ],
        compiler_params=PARAMS,
        name="code_mass",
    )(me, codebook, all_lse, *pieces)


def rows_call(me, encoded, codebook, row_lse, shift, gathered, devices, own):
    rows, features = encoded.shape
    codes = codebook.shape[0]
    span = math.gcd(devices, max(1, 8192 // own))
    block = span * own
    chunk = math.gcd(own, 512)

    def kernel(me_ref, encoded_ref, codes_ref, lse_ref, shift_ref, vectors_ref, out_ref, lse_wide, shift_wide):
        step = pl.program_id(0)

        @pl.when(step == 0)
        def _():
            out_ref[...] = jnp.zeros(out_ref.shape, jnp.float32)
            mine = pl.ds(pl.multiple_of(me_ref[0] * rows, rows), rows)
            lse_wide[...] = row_to_columns(lse_ref[...])
            shift_wide[...] = row_to_columns(shift_ref[:, mine])

        encoded_here = encoded_ref[...]
        total = out_ref[...]
        for k in range(block // chunk):
            code_rows = codes_ref[k * chunk : (k + 1) * chunk, :]
            scores = lax.dot_general(encoded_here, code_rows, NT, preferred_element_type=jnp.float32)
            owner, start = divmod(k * chunk, own)
            place = place_of(me_ref[0] ^ (step * span + owner), devices)
            log_mass = vectors_ref[place, :, start : start + chunk]
            squares = vectors_ref[place, :, own + start : own + start + chunk]
            tiles = []
            for q in range(chunk // LANES):
                lane = slice(q * LANES, (q + 1) * LANES)
                logits = scores[:, lane] * LOG2E - squares[:, lane] - lse_wide[...]
                tile = jnp.exp2(logits) * (log_mass[:, lane] - logits + shift_wide[...])
                tiles.append(tile.astype(jnp.bfloat16))
            grad_tile = jnp.concatenate(tiles, axis=1)
            total = total + jnp.dot(grad_tile, code_rows, preferred_element_type=jnp.float32)
        out_ref[...] = total

    return pl.pallas_call(
        kernel,
        grid_spec=pltpu.PrefetchScalarGridSpec(
            num_scalar_prefetch=1,
            grid=(codes // block,),
            in_specs=[
                pl.BlockSpec((rows, features), lambda i, me: (0, 0)),
                pl.BlockSpec((block, features), lambda i, me: (i, 0)),
                pl.BlockSpec(row_lse.shape, lambda i, me: (0, 0)),
                pl.BlockSpec(shift.shape, lambda i, me: (0, 0)),
                pl.BlockSpec((devices, 1, 2 * own), lambda i, me: (0, 0, 0)),
            ],
            out_specs=pl.BlockSpec((rows, features), lambda i, me: (0, 0)),
            scratch_shapes=[pltpu.VMEM((rows, LANES), jnp.float32)] * 2,
        ),
        out_shape=jax.ShapeDtypeStruct((rows, features), jnp.float32),
        compiler_params=PARAMS,
        name="grad_rows",
    )(me, encoded, codebook, row_lse, shift, gathered)


def codes_call(me, pieces, codebook, all_lse, shift, log_mass, squares, devices, own):
    rows, features = pieces[0].shape
    block = math.gcd(own, 1024)
    blocks = own // block

    def kernel(me_ref, codes_ref, lse_ref, shift_ref, log_ref, squares_ref, *refs):
        row_refs, out_ref = refs[:-1], refs[-1]
        log_mass = row_to_columns(log_ref[0])
        half = row_to_columns(squares_ref[0])
        code_rows = codes_ref[...]
        total = jnp.zeros((block, features), jnp.float32)
        sums = jnp.zeros((block, LANES), jnp.float32)
        for p in range(devices):
            piece, start = piece_of(p, rows)
            row_block = row_refs[piece][start : start + rows, :]
            scores = lax.dot_general(code_rows, row_block, NT, preferred_element_type=jnp.float32)
            there = pl.ds(pl.multiple_of((me_ref[0] ^ place_of(p, devices)) * rows, rows), rows)
            shift_here = shift_ref[:, there]
            tiles = []
            for q in range(rows // LANES):
                lane = slice(q * LANES, (q + 1) * LANES)
                logits = scores[:, lane] * LOG2E - half - lse_ref[p, :, lane]
                tile = jnp.exp2(logits) * (log_mass - logits + shift_here[:, lane])
                sums = sums + tile
                tiles.append(tile.astype(jnp.bfloat16))
            grad_tile = jnp.concatenate(tiles, axis=1)
            total = total + jnp.dot(grad_tile, row_block, preferred_element_type=jnp.float32)
        code_sums = jnp.sum(sums, axis=1, keepdims=True)
        out_ref[...] = total - code_sums * code_rows.astype(jnp.float32)

    return pl.pallas_call(
        kernel,
        grid_spec=pltpu.PrefetchScalarGridSpec(
            num_scalar_prefetch=1,
            grid=(blocks,),
            in_specs=[
                pl.BlockSpec((block, features), lambda i, me: (me[0] * blocks + i, 0)),
                pl.BlockSpec((devices, 1, rows), lambda i, me: (0, 0, 0)),
                pl.BlockSpec((1, rows * devices), lambda i, me: (0, 0)),
                pl.BlockSpec((1, 1, block), lambda i, me: (0, 0, i)),
                pl.BlockSpec((1, 1, block), lambda i, me: (0, 0, i)),
            ]
            + [pl.BlockSpec(piece.shape, lambda i, me: (0, 0)) for piece in pieces],
            out_specs=pl.BlockSpec((block, features), lambda i, me: (i, 0)),
        ),
        out_shape=jax.ShapeDtypeStruct((own, features), jnp.float32),
        compiler_params=PARAMS,
        name="grad_codes",
    )(me, codebook, all_lse, shift, log_mass, squares, *pieces)


def from_xor(values, axis, offset):
    return lax.ppermute(values, axis, [(i, i ^ offset) for i in range(lax.axis_size(axis))])


def xor_gather(held, axis):
    offset = lax.axis_size(axis) // 2
    while offset:
        held = jnp.concatenate([held, from_xor(held, axis, offset)], axis=0)
        offset //= 2
    return held


def xor_sum(values, axis):
    offset = lax.axis_size(axis) // 2
    while offset:
        values = values + from_xor(values, axis, offset)
        offset //= 2
    return values


def body(encoded, codebook):
    rows, features = encoded.shape
    codes = codebook.shape[0]
    devices = lax.axis_size("dp")
    own = codes // devices
    me = lax.axis_index("dp").astype(jnp.int32).reshape(1)
    offsets = [devices >> (k + 1) for k in range(devices.bit_length() - 1)]

    pieces = [encoded]

    def gather_more(after):
        if len(pieces) > len(offsets):
            return after
        held, after = lax.optimization_barrier((tuple(pieces), after))
        pieces[:] = held
        joined = lax.optimization_barrier(jnp.concatenate(pieces, axis=0)) if len(pieces) > 1 else encoded
        pieces.append(from_xor(joined, "dp", offsets[len(pieces) - 1]))
        return after

    state = jnp.stack([jnp.full((8, rows), -3e38, jnp.float32), jnp.zeros((8, rows), jnp.float32)])
    state = gather_more(state)
    state = stats_call(encoded, codebook, state, 0, codes // 2)
    state = gather_more(state)
    stats = stats_call(encoded, codebook, state, codes // 2, codes)
    stats = gather_more(stats)
    offset = lax.axis_size("code") // 2
    while offset:
        other = from_xor(stats, "code", offset)
        top = jnp.maximum(stats[0:1], other[0:1])
        total = stats[1:2] * jnp.exp2(stats[0:1] - top) + other[1:2] * jnp.exp2(other[0:1] - top)
        stats = jnp.concatenate([top, total], axis=0)
        offset //= 2
    row_lse = stats[0:1] + jnp.log2(stats[1:2]) - LOG2LN2
    all_lse = lax.optimization_barrier(row_lse[None])
    for k, offset in enumerate(offsets):
        all_lse = jnp.concatenate([all_lse, from_xor(all_lse, "dp", offset)], axis=0)
        if k:
            all_lse = gather_more(all_lse)

    log_mass, squares, cross = mass_call(me, pieces, codebook, all_lse, devices, own)
    offset = lax.axis_size("code") // 2
    while offset > 1:
        cross = cross + from_xor(cross, "code", offset)
        offset //= 2
    message = jnp.concatenate([log_mass, squares, cross[None]], axis=2)
    if offset:
        message = message + jnp.pad(from_xor(cross, "code", offset)[None], ((0, 0), (0, 0), (2 * own, 0)))
    gathered = xor_gather(lax.optimization_barrier(message), "dp")
    shift = jnp.sum(gathered[:, :, 2 * own :], axis=0) * (-1.0 / LN2)

    local_rows = rows_call(me, encoded, codebook, row_lse, shift, gathered, devices, own)
    grad_codes = codes_call(me, pieces, codebook, all_lse, shift, log_mass, squares, devices, own)
    grad_rows = xor_sum(local_rows, "code")
    return grad_rows, grad_codes


def solution(mesh):
    placed = (P("dp", None), P("code", None))
    return jax.shard_map(
        body,
        mesh=mesh,
        in_specs=placed,
        out_specs=(P("dp", None), P(("code", "dp"), None)),
        check_vma=False,
    )
```
